32 devices in a mesh: dp: 16 (over z, y, x), rep: 2 (over core).
Axes of the slice: x: 2, y: 2, z: 4, core: 2. Of those that a mesh axis runs over, the one named last changes fastest.
Arguments:
- images: bfloat16 [2, 512, 16, 512], P(None, ('dp', 'rep')), may hold values from -6 to 6
- lengths: int32 [2, 7], replicated, may hold values from 1 to 128, 256 in all within a row
- widths: int32 [2, 7], replicated, may hold values from 8 to 16
- conv_one: bfloat16 [3, 3, 512, 512], P(None, None, 'dp'), may hold values from -0.09375 to 0.09375
- conv_two: bfloat16 [3, 3, 512, 512], P(None, None, 'dp'), may hold values from -0.09375 to 0.09375
- squeeze: bfloat16 [3, 512, 128], P(None, 'dp'), may hold values from -0.25 to 0.25
- expand: bfloat16 [3, 128, 512], P(None, 'dp'), may hold values from -0.5 to 0.5
- task_conv: bfloat16 [3, 3, 3, 512, 512], P(None, None, None, 'dp'), may hold values from -0.09375 to 0.09375
- gains_shared: float32 [2, 512], replicated, may hold values from 0.25 to 1.75
- biases_shared: float32 [2, 512], replicated, may hold values from -2.5 to 2.5
- gains_squeeze: float32 [3, 128], replicated, may hold values from 0.25 to 1.75
- biases_squeeze: float32 [3, 128], replicated, may hold values from -2.5 to 2.5
- gains_expand: float32 [3, 512], replicated, may hold values from 0.25 to 1.75
- biases_expand: float32 [3, 512], replicated, may hold values from -2.5 to 2.5
- gains_task: float32 [3, 512], replicated, may hold values from 0.25 to 1.75
- biases_task: float32 [3, 512], replicated, may hold values from -2.5 to 2.5
- loss_history: float32 [3, 2], replicated, may hold values from 0.5 to 2
- cotangent: bfloat16 [3, 2, 256, 8, 512], P(None, None, ('dp', 'rep')), may hold values from -6 to 6
Outputs:
- features: float32 [3, 2, 256, 8, 512], P(None, None, ('dp', 'rep'))
- input_grad: float32 [2, 512, 16, 512], P(None, ('dp', 'rep'))
- grad_conv_one: float32 [3, 3, 512, 512], P(None, None, 'dp')
- grad_conv_two: float32 [3, 3, 512, 512], P(None, None, 'dp')
- grad_squeeze: float32 [3, 512, 128], P(None, 'dp')
- grad_expand: float32 [3, 128, 512], P(None, 'dp')
- grad_task_conv: float32 [3, 3, 3, 512, 512], P(None, None, None, 'dp')
- grad_gains_shared: float32 [2, 512], replicated
- grad_biases_shared: float32 [2, 512], replicated
- grad_gains_squeeze: float32 [3, 128], replicated
- grad_biases_squeeze: float32 [3, 128], replicated
- grad_gains_expand: float32 [3, 512], replicated
- grad_biases_expand: float32 [3, 512], replicated
- grad_gains_task: float32 [3, 512], replicated
- grad_biases_task: float32 [3, 512], replicated
The draws below stay inside these ranges and needn't reach their ends.
Inputs may be any that keep to these rules, and one draw needn't show every extreme that they name: `lengths`: the 7 entries of a micro-batch sum to 256 and the largest equals 128; an image's height is twice its entry. `widths`: columns from an image's width on are padding.
All inputs are finite; a program needn't handle non-finite values.
Results may differ from the reference program's by a relative error of at most 0.015.
Values may be sent and summed in bfloat16 or wider, within the bound.
No kernel may reach another device: no remote copies, remote signals or barrier semaphores. Data moves between devices by JAX's collectives and lax.ppermute only.
A program may use at most 256 MiB of HBM per device.

```python
import math
import jax
import jax.numpy as jnp
import numpy as np
from jax import lax

C = 512
B = 128
TASKS = 3
IMAGES = 7
MICRO = 2
WIDTH = 16
ROWS = 512


def place_ends(array, own_key, low, top_value):
    longest = array.shape.index(max(array.shape))
    spots = []
    for shift in (0, 1):
        where = [jax.random.randint(jax.random.fold_in(own_key, axis), (), 0, length) for axis, length in enumerate(array.shape)]
        where[longest] = (where[longest] + shift) % array.shape[longest]
        spots.append(tuple(where))
    return array.at[spots[0]].set(low).at[spots[1]].set(top_value)


def shard_levels(key, dims, pieces, low, largest):
    def one(axis_at, blocks):
        heights = jax.random.uniform(jax.random.fold_in(jax.random.fold_in(key, 6), axis_at), (blocks,), jnp.float32, low / len(pieces), largest / len(pieces))
        return jnp.repeat(jnp.exp(heights), dims[axis_at] // blocks).reshape((-1,) + (1,) * (len(dims) - axis_at - 1))

    level = one(*pieces[0])
    for cut in pieces[1:]:
        level = level * one(*cut)
    return level


def profile(count, total, reach, skew):
    weights = [(1 << 20) // math.isqrt(grade ** skew) + 1 for grade in range(2, count + 1)]
    surplus, counts = total - reach - (count - 1), [1] * (count - 1)
    while surplus > 0:
        movable = [i for i in range(count - 1) if counts[i] < reach]
        whole, left = sum([weights[i] for i in movable]), surplus
        for i in movable:
            extra = min(reach - counts[i], max(1, left * weights[i] // whole), surplus)
            counts[i] = counts[i] + extra
            surplus = surplus - extra
    return np.array([reach] + counts)


def ragged_sizes(own_key, count, total, reach, slope):
    if count == 2:
        one = jax.random.randint(own_key, (), max(1, total - reach), min(reach, total - 1) + 1)
        return jnp.stack([one, total - one])
    sizes = jnp.asarray(profile(count, total, reach, slope), jnp.int32)
    twos = (count - 1) // 2
    donor, receiver = sizes[1:1 + 2 * twos:2], sizes[2:2 + 2 * twos:2]
    margin = jnp.minimum(donor - 1, reach - receiver)
    moved = jax.random.randint(jax.random.fold_in(own_key, 1), (twos,), 0, 1 << 20) % (margin + 1)
    sizes = sizes.at[1:1 + 2 * twos:2].set(donor - moved).at[2:2 + 2 * twos:2].set(receiver + moved)
    return sizes[jax.random.permutation(jax.random.fold_in(own_key, 2), count)]


def bell_draw(rng, dims, scale, bound, split=(), kind=jnp.bfloat16):
    values = scale * jax.random.normal(rng, dims, jnp.float32)
    if split:
        values = values * shard_levels(rng, dims, split, -0.22, 0.18)
    return jnp.clip(values, -bound, bound).astype(kind)


def setup_inputs(seed: int = 0) -> dict:
    keys = jax.random.split(jax.random.key(seed), 19)
    images = bell_draw(keys[0], (MICRO, ROWS, WIDTH, C), 1.0, 6.0, ((1, 32),))
    lengths = jax.vmap(lambda own: ragged_sizes(own, IMAGES, ROWS // 2, ROWS // 4, 2))(jax.random.split(keys[1], MICRO)).reshape((MICRO, IMAGES)).astype(jnp.int32)
    widths = place_ends(jax.random.randint(keys[2], (MICRO, IMAGES), WIDTH // 2, WIDTH + 1), jax.random.fold_in(keys[2], 1), WIDTH // 2, WIDTH).astype(jnp.int32)
    conv_one = bell_draw(keys[3], (3, 3, C, C), (9 * C) ** -0.5, 0.09375, ((2, 16),))
    conv_two = bell_draw(keys[4], (3, 3, C, C), (9 * C) ** -0.5, 0.09375, ((2, 16),))
    squeeze = bell_draw(keys[5], (TASKS, C, B), C ** -0.5, 0.25, ((1, 16),))
    expand = bell_draw(keys[6], (TASKS, B, C), B ** -0.5, 0.5, ((1, 16),))
    task_conv = bell_draw(keys[7], (TASKS, 3, 3, C, C), (9 * C) ** -0.5, 0.09375, ((3, 16),))
    gains_shared = jnp.clip(1.0 + 0.15 * jax.random.normal(keys[8], (2, C), jnp.float32), 0.25, 1.75)
    biases_shared = bell_draw(keys[9], (2, C), 0.5, 2.5, (), jnp.float32)
    gains_squeeze = jnp.clip(1.0 + 0.15 * jax.random.normal(keys[10], (TASKS, B), jnp.float32), 0.25, 1.75)
    biases_squeeze = bell_draw(keys[11], (TASKS, B), 0.5, 2.5, (), jnp.float32)
    gains_expand = jnp.clip(1.0 + 0.15 * jax.random.normal(keys[12], (TASKS, C), jnp.float32), 0.25, 1.75)
    biases_expand = bell_draw(keys[13], (TASKS, C), 0.5, 2.5, (), jnp.float32)
    gains_task = jnp.clip(1.0 + 0.15 * jax.random.normal(keys[14], (TASKS, C), jnp.float32), 0.25, 1.75)
    biases_task = bell_draw(keys[15], (TASKS, C), 0.5, 2.5, (), jnp.float32)
    loss_history = jnp.clip(jnp.exp(jax.random.uniform(keys[16], (TASKS, 2), jnp.float32, math.log(0.5), math.log(2.0))), 0.5, 2.0)
    cotangent = bell_draw(keys[17], (TASKS, MICRO, ROWS // 2, WIDTH // 2, C), 1.0, 6.0, ((2, 32),))
    return dict(images=images, lengths=lengths, widths=widths, conv_one=conv_one, conv_two=conv_two, squeeze=squeeze, expand=expand, task_conv=task_conv, gains_shared=gains_shared, biases_shared=biases_shared, gains_squeeze=gains_squeeze, biases_squeeze=biases_squeeze, gains_expand=gains_expand, biases_expand=biases_expand, gains_task=gains_task, biases_task=biases_task, loss_history=loss_history, cotangent=cotangent)


EPSILON = 1e-05
EXACT = lax.Precision.HIGHEST

@jax.custom_vjp
def low(v):
    return lax.optimization_barrier(v.astype(jnp.bfloat16)).astype(jnp.float32)

@jax.custom_vjp
def low_back(v):
    return v

def low_keep(v):
    return (low(v), None)

def low_pass(kept, grad):
    return (grad,)

def back_keep(v):
    return (v, None)

def back_low(kept, grad):
    return (low(grad),)
low.defvjp(low_keep, low_pass)
low_back.defvjp(back_keep, back_low)

def layout(length_row, width_row, offset, row_count, col_count):
    image_count = length_row.shape[0]
    image_ends = 2 * jnp.cumsum(length_row)
    starts = image_ends - 2 * length_row
    places = offset + jnp.arange(row_count + 1, dtype=jnp.int32)
    image_index = lax.optimization_barrier(jnp.sum((places[:, None] >= image_ends[None, :]).astype(jnp.int32), axis=1))
    member = (image_index[:, None] == jnp.arange(image_count, dtype=jnp.int32)[None, :]).astype(jnp.int32)
    first_row = lax.optimization_barrier(jnp.sum((places[:, None] == starts[None, :]).astype(jnp.float32), axis=1))
    linked = 1.0 - first_row
    row_width = lax.optimization_barrier(jnp.sum(member * width_row[None, :], axis=1))
    columns = jnp.arange(col_count, dtype=jnp.int32)
    pixel_mask = (columns[None, :] < row_width[:row_count, None]).astype(jnp.float32)
    return (pixel_mask, linked[:row_count], linked[1:])

def conv_single(activation, weight, up_flag, down_flag):
    row_count = activation.shape[0]
    col_count = activation.shape[1]
    padded = jnp.pad(activation, ((1, 1), (1, 1), (0, 0)))
    factors = (up_flag, jnp.ones_like(up_flag), down_flag)
    running_total = jnp.zeros((row_count, col_count, weight.shape[3]), jnp.float32)
    for tap_row in range(3):
        partial_sum = jnp.zeros((row_count, col_count, weight.shape[3]), jnp.float32)
        for tap_col in range(3):
            piece = padded[tap_row:tap_row + row_count, tap_col:tap_col + col_count]
            partial_sum = partial_sum + jnp.einsum('rwc,cd->rwd', piece, weight[tap_row, tap_col], precision=EXACT)
        running_total = running_total + factors[tap_row][:, None, None] * partial_sum
    return running_total

def convolve(activation, weight, up_flag, down_flag):

    def single(batch_items):
        return conv_single(batch_items[0], batch_items[1], up_flag, down_flag)
    return lax.map(jax.checkpoint(single), (activation, weight))

def batch_norm(values, valid_mask, gain_row, shift_row):
    pixel_count = jnp.sum(valid_mask)
    center = lax.optimization_barrier(jnp.sum(values * valid_mask, axis=(1, 2), keepdims=True)) / pixel_count
    spread = lax.optimization_barrier(jnp.sum(valid_mask * (values - center) ** 2, axis=(1, 2), keepdims=True)) / pixel_count
    return gain_row[:, None, None, :] * (values - center) * lax.rsqrt(spread + EPSILON) + shift_row[:, None, None, :]

def micro_forward(picture, length_row, width_row, params):
    weight_one, weight_two, weight_squeeze, weight_expand, weight_task, gain_shared, shift_shared, gain_squeeze, shift_squeeze, gain_expand, shift_expand, gain_task, shift_task = params
    pixel_mask, up_flag, down_flag = layout(length_row, width_row, 0, ROWS, WIDTH)
    valid_mask = pixel_mask[None, :, :, None]
    entering = low(valid_mask * picture[None])
    conv_first = low_back(convolve(entering, weight_one[None], up_flag, down_flag))
    hidden_one = low(valid_mask * jax.nn.silu(batch_norm(conv_first, valid_mask, gain_shared[0:1], shift_shared[0:1])))
    conv_second = low_back(convolve(hidden_one, weight_two[None], up_flag, down_flag))
    shared = valid_mask * jax.nn.silu(batch_norm(conv_second, valid_mask, gain_shared[1:2], shift_shared[1:2]))
    shared_low = low(shared)
    squeezed = low_back(jnp.einsum('rwc,tcb->trwb', shared_low[0], weight_squeeze, precision=EXACT))
    narrow = low(valid_mask * jax.nn.silu(batch_norm(squeezed, valid_mask, gain_squeeze, shift_squeeze)))
    expanded = low_back(jnp.einsum('trwb,tbc->trwc', narrow, weight_expand, precision=EXACT))
    attention = valid_mask * jax.nn.sigmoid(batch_norm(expanded, valid_mask, gain_expand, shift_expand))
    gated_low = low(attention * shared)
    task_out = low_back(convolve(gated_low, weight_task, up_flag, down_flag))
    finished = valid_mask * jax.nn.silu(batch_norm(task_out, valid_mask, gain_task, shift_task))
    shaped = finished.reshape(TASKS, ROWS // 2, 2, WIDTH // 2, 2, finished.shape[3])
    return 0.25 * lax.optimization_barrier(jnp.sum(shaped, axis=(2, 4)))

def reference(images, lengths, widths, conv_one, conv_two, squeeze, expand, task_conv, gains_shared, biases_shared, gains_squeeze, biases_squeeze, gains_expand, biases_expand, gains_task, biases_task, loss_history, cotangent):

    def forward(pictures, weight_one, weight_two, weight_squeeze, weight_expand, weight_task, gain_shared, shift_shared, gain_squeeze, shift_squeeze, gain_expand, shift_expand, gain_task, shift_task):
        params = (weight_one, weight_two, weight_squeeze, weight_expand, weight_task, gain_shared, shift_shared, gain_squeeze, shift_squeeze, gain_expand, shift_expand, gain_task, shift_task)

        def one_batch(batch_items):
            return micro_forward(batch_items[0], batch_items[1], batch_items[2], params)
        pooled = lax.map(jax.checkpoint(one_batch), (pictures, lengths, widths))
        return jnp.transpose(pooled, (1, 0, 2, 3, 4))
    inputs = (images.astype(jnp.float32), conv_one.astype(jnp.float32), conv_two.astype(jnp.float32), squeeze.astype(jnp.float32), expand.astype(jnp.float32), task_conv.astype(jnp.float32), gains_shared, biases_shared, gains_squeeze, biases_squeeze, gains_expand, biases_expand, gains_task, biases_task)
    features, pullback = jax.vjp(forward, *inputs)
    loss_ratio = loss_history[:, 1] / loss_history[:, 0]
    task_scale = TASKS * jax.nn.softmax(loss_ratio / 2.0)
    gradients = pullback(task_scale[:, None, None, None, None] * cotangent.astype(jnp.float32))
    return (features, gradients[0], gradients[1], gradients[2], gradients[3], gradients[4], gradients[5], gradients[6], gradients[7], gradients[8], gradients[9], gradients[10], gradients[11], gradients[12], gradients[13])
```

```python
import functools
import math

import jax
import jax.numpy as jnp
from jax import lax
from jax.experimental import pallas as pl
from jax.experimental.pallas import tpu as pltpu
from jax.sharding import PartitionSpec as P

EPSILON = 1e-05
AXES = ("dp", "rep")
F32 = jnp.float32
BF16 = jnp.bfloat16
BLOCKS = 16
NEAR = 256 * 1024
FAR = 750000
SPARE = 8 * 1024 * 1024


class Sizes:
    def __init__(self, batches, rows, cols, channels, tasks):
        self.batches, self.rows, self.cols, self.channels = batches, rows, cols, channels
        self.tasks = tasks
        self.own = rows * cols
        self.ext = (rows + 2) * cols
        self.half = channels // 2
        self.block = channels // BLOCKS


def whole(_=None):
    return pl.BlockSpec(memory_space=pltpu.VMEM)


def scalars():
    return pl.BlockSpec(memory_space=pltpu.SMEM)


def in_place():
    return pl.BlockSpec(memory_space=pltpu.HBM)


def unread():
    return pl.BlockSpec(memory_space=pl.ANY)


def per_task(*shape):
    return pl.BlockSpec((1, *shape), lambda t: (t, *(0 for _ in shape)))


def row_of(index, size):
    return pl.ds(pl.multiple_of(index * size, size), size)


def columns_of(s):
    return lax.broadcasted_iota(jnp.int32, (s.cols, s.channels), 0)


def width_at(tab, s, m, i):
    return tab[m * (s.rows + 2) + i]


def link_at(tab, s, m, r):
    return tab[s.batches * (s.rows + 2) + m * (s.rows + 1) + r].astype(F32)


def logistic(v):
    return 0.5 + 0.5 * jnp.tanh(0.5 * v)


def silu_slope(v):
    q = logistic(v)
    return q * (1.0 + v * (1.0 - q))


class Norm:
    def __init__(self, coef, back, m, batches):
        self.mean = coef[pl.ds(m, 1), :]
        self.inverse = coef[pl.ds(batches + m, 1), :]
        self.gain = coef[pl.ds(2 * batches + m, 1), :]
        self.shift = coef[pl.ds(3 * batches + m, 1), :]
        if back is not None:
            self.back_shift = back[pl.ds(m, 1), :]
            self.back_gain = back[pl.ds(batches + m, 1), :]

    def scaled(self, z):
        return (z - self.mean) * self.inverse

    def level(self, scaled):
        return self.gain * scaled + self.shift

    def grad(self, dy, scaled):
        return self.gain * self.inverse * (dy - self.back_shift - scaled * self.back_gain)


def stage(s, x_ref, up, own, down):
    col = columns_of(s)
    for m in range(s.batches):

        def put(i, x, m=m):
            at = ext_slice(s, m, i)
            before = jnp.where(col > 0, pltpu.roll(x, 1, 0), 0.0)
            behind = jnp.where(col < s.cols - 1, pltpu.roll(x, s.cols - 1, 0), 0.0)
            x_ref[at, : s.channels] = before.astype(BF16)
            x_ref[at, s.channels : 2 * s.channels] = x.astype(BF16)
            x_ref[at, 2 * s.channels :] = behind.astype(BF16)

        put(0, up(m))
        put(s.rows + 1, down(m))

        def middle(r, m=m, put=put):
            put(r + 1, own(m, r))

        by_groups(s.rows, middle)


def by_groups(count, body):
    size = 4 if count % 4 == 0 else 2

    def step(i, carry):
        for j in range(size):
            body(size * i + j)
        return carry

    lax.fori_loop(0, count // size, step, 0)


def own_slice(s, m, r):
    return pl.ds(pl.multiple_of(m * s.own + r * s.cols, s.cols), s.cols)


def ext_slice(s, m, i):
    return pl.ds(pl.multiple_of(m * s.ext + i * s.cols, s.cols), s.cols)


def each_row(s, body):
    for m in range(s.batches):
        by_groups(s.rows, functools.partial(body, m))


def span_of(s):
    return s.batches * s.ext - 2 * s.cols


def product(s, x_ref, w_ref, p_ref, flipped):
    def part(a, carry):
        rows = pl.ds(pl.multiple_of(a * s.cols, s.cols), span_of(s))
        if flipped:
            total = None
            for b in range(3):
                term = lax.dot_general(
                    x_ref[rows, b * s.channels : (b + 1) * s.channels],
                    w_ref[8 - (3 * a + b)],
                    (((1,), (1,)), ((), ())),
                    preferred_element_type=F32,
                )
                total = term if total is None else total + term
        else:
            taps = w_ref[pl.ds(3 * a, 3)].reshape(3 * s.channels, s.channels)
            total = jnp.dot(x_ref[rows, :], taps, preferred_element_type=F32)
        p_ref[a] = total
        return carry

    lax.fori_loop(0, 3, part, 0)


def combined(s, tab, p_ref, m, r):
    at = ext_slice(s, m, r)
    up, down = link_at(tab, s, m, r), link_at(tab, s, m, r + 1)
    return p_ref[1, at, :] + up * p_ref[0, at, :] + down * p_ref[2, at, :]


def put_statistics(s, tab, load, st_ref):
    col = columns_of(s)
    zero = jnp.zeros((s.cols, s.channels), F32)
    for m in range(s.batches):
        first = width_at(tab, s, m, 1)
        start = jnp.sum(jnp.where(col < first, load(m, 0), 0.0), axis=0, keepdims=True)
        center = start / first.astype(F32)

        def step(i, totals, m=m, center=center):
            for r in (2 * i, 2 * i + 1):
                off = jnp.where(col < width_at(tab, s, m, r + 1), load(m, r) - center, 0.0)
                totals = (totals[0] + off, totals[1] + off * off)
            return totals

        totals = lax.fori_loop(0, s.rows // 2, step, (zero, zero))
        total = jnp.sum(totals[0], axis=0, keepdims=True)
        spread = jnp.sum(totals[1], axis=0, keepdims=True)
        count = first
        for r in range(1, s.rows):
            count = count + width_at(tab, s, m, r + 1)
        count = count.astype(F32)
        st_ref[pl.ds(m, 1), :] = total + count * center
        st_ref[pl.ds(s.batches + m, 1), :] = jnp.maximum(spread - total * total / count, 0.0)


def put_gradients(s, st_ref, load):
    zero = jnp.zeros((s.cols, s.channels), F32)
    for m in range(s.batches):

        def step(i, totals, m=m):
            for r in (2 * i, 2 * i + 1):
                dy, scaled = load(m, r)
                totals = (totals[0] + dy, totals[1] + dy * scaled)
            return totals

        totals = lax.fori_loop(0, s.rows // 2, step, (zero, zero))
        st_ref[pl.ds(m, 1), :] = jnp.sum(totals[0], axis=0, keepdims=True)
        st_ref[pl.ds(s.batches + m, 1), :] = jnp.sum(totals[1], axis=0, keepdims=True)


def put_edges(s, src_ref, up_ref, down_ref):
    for m in range(s.batches):
        up_ref[pl.ds(m * s.cols, s.cols), :] = src_ref[pl.ds(m * s.own, s.cols), :]
        down_ref[pl.ds(m * s.cols, s.cols), :] = src_ref[
            pl.ds((m + 1) * s.own - s.cols, s.cols), :
        ]


def fetch(s, pieces, slots, w_ref, sem, first, count):
    copies = []
    for piece in pieces:
        for j in range(piece.shape[0]):
            at = len(copies)
            block, half = slots[at], slots[2 * BLOCKS + at // BLOCKS]
            copies.append(
                pltpu.make_async_copy(
                    piece.at[j, pl.ds(first, count)],
                    w_ref.at[:, row_of(block, s.block), row_of(half, s.half)],
                    sem.at[at],
                )
            )
    return copies


def start_all(copies):
    for copy in copies:
        copy.start()


def wait_all(copies):
    for copy in copies:
        copy.wait()


def conv_one_kernel(
    s, tab, slots, img, img_up, img_down, p0, p1, p2, p3, z, st, eu, ed, x, p, w, sem
):
    copies = fetch(s, (p0, p1, p2, p3), slots, w, sem, 0, 9)
    start_all(copies)
    col = columns_of(s)

    def valid(row, m, i):
        return jnp.where(col < width_at(tab, s, m, i), row.astype(F32), 0.0)

    stage(
        s,
        x,
        lambda m: valid(img_up[pl.ds(m * s.cols, s.cols), :], m, 0),
        lambda m, r: valid(img[own_slice(s, m, r), :], m, r + 1),
        lambda m: valid(img_down[pl.ds(m * s.cols, s.cols), :], m, s.rows + 1),
    )
    wait_all(copies)
    convolved(s, tab, x, w, p, z, st, eu, ed)


def convolved(s, tab, x, w, p, z, st, eu, ed):
    product(s, x, w, p, False)

    def row(m, r):
        y = combined(s, tab, p, m, r)
        z[own_slice(s, m, r), :] = y
        return y

    put_statistics(s, tab, row, st)
    put_edges(s, z, eu, ed)


def conv_two_kernel(
    s, tab, slots, z1, zu, zd, coef, p0, p1, z, st, eu, ed, h1, x, p, w, sem
):
    copies = fetch(s, (p0, p1), slots, w, sem, 0, 9)
    start_all(copies)
    col = columns_of(s)
    norms = [Norm(coef, None, m, s.batches) for m in range(s.batches)]

    def active(row, m, i):
        level = norms[m].level(norms[m].scaled(row))
        y = jnp.where(col < width_at(tab, s, m, i), level * logistic(level), 0.0)
        return y.astype(BF16).astype(F32)

    def own(m, r):
        y = active(z1[own_slice(s, m, r), :], m, r + 1)
        h1[own_slice(s, m, r), :] = y.astype(BF16)
        return y

    stage(
        s,
        x,
        lambda m: active(zu[pl.ds(m * s.cols, s.cols), :], m, 0),
        own,
        lambda m: active(zd[pl.ds(m * s.cols, s.cols), :], m, s.rows + 1),
    )
    wait_all(copies)
    convolved(s, tab, x, w, p, z, st, eu, ed)


def squeeze_kernel(s, tab, slots, z2, zu, zd, coef, p0, p1, shared, a, st, low, w, sem):
    copies = fetch(s, (p0, p1), slots, w, sem, 9, 1)
    start_all(copies)
    col = columns_of(s)
    for m in range(s.batches):
        norm = Norm(coef, None, m, s.batches)

        def active(x, i, m=m, norm=norm):
            level = norm.level(norm.scaled(x))
            y = jnp.where(col < width_at(tab, s, m, i), level * logistic(level), 0.0)
            shared[ext_slice(s, m, i), :] = y
            low[ext_slice(s, m, i), :] = y.astype(BF16)

        active(zu[pl.ds(m * s.cols, s.cols), :], 0)
        active(zd[pl.ds(m * s.cols, s.cols), :], s.rows + 1)

        def step(r, m=m, active=active):
            active(z2[own_slice(s, m, r), :], r + 1)

        by_groups(s.rows, step)
    wait_all(copies)
    a[...] = jnp.dot(low[...], w[0], preferred_element_type=F32)
    put_statistics(s, tab, lambda m, r: a[ext_slice(s, m, r + 1), :], st)


def lane_task(s, shape, dim):
    return (lax.broadcasted_iota(jnp.int32, shape, dim) // 8) % 4


def expand_kernel(s, tab, slots, a, coef, p0, p1, e, st, narrow, low, w, sem):
    t = pl.program_id(0)
    copies = fetch(s, (p0, p1), slots, w, sem, 10, 1)

    @pl.when(t == 0)
    def _():
        start_all(copies)
        col = columns_of(s)
        for m in range(s.batches):
            norm = Norm(coef, None, m, s.batches)

            def step(i, m=m, norm=norm):
                level = norm.level(norm.scaled(a[ext_slice(s, m, i), :]))
                y = jnp.where(col < width_at(tab, s, m, i), level * logistic(level), 0.0)
                low[ext_slice(s, m, i), :] = y.astype(BF16)

            by_groups(s.rows + 2, step)
            narrow[pl.ds(m * s.own, s.own), :] = low[pl.ds(m * s.ext + s.cols, s.own), :]
        wait_all(copies)

    mine = lane_task(s, (s.batches * s.ext, s.channels), 1) == t
    chosen = jnp.where(mine, low[...].astype(F32), 0.0).astype(BF16)
    e[0] = jnp.dot(chosen, w[0], preferred_element_type=F32)
    put_statistics(s, tab, lambda m, r: e[0, ext_slice(s, m, r + 1), :], st.at[0])


def task_kernel(
    s, tab, slots, e, shared, coef, *refs
):
    pieces, (k, st, eu, ed, gated, x, p, w, sem) = refs[:-9], refs[-9:]
    t = pl.program_id(0)

    def copies(task):
        return fetch(s, pieces, slots, w.at[task % 2], sem.at[task % 2], 9 * task, 9)

    @pl.when(t == 0)
    def _():
        start_all(copies(0))

    @pl.when(t + 1 < s.tasks)
    def _():
        start_all(copies(t + 1))

    col = columns_of(s)
    norms = [Norm(coef.at[0], None, m, s.batches) for m in range(s.batches)]

    def active(m, i):
        level = norms[m].level(norms[m].scaled(e[0, ext_slice(s, m, i), :]))
        att = jnp.where(col < width_at(tab, s, m, i), logistic(level), 0.0)
        return (att * shared[ext_slice(s, m, i), :]).astype(BF16).astype(F32)

    def own(m, r):
        y = active(m, r + 1)
        gated[0, own_slice(s, m, r), :] = y.astype(BF16)
        return y

    stage(s, x, lambda m: active(m, 0), own, lambda m: active(m, s.rows + 1))
    wait_all(copies(t))
    convolved(s, tab, x, w.at[t % 2], p, k.at[0], st.at[0], eu.at[0], ed.at[0])


def task_slope_kernel(
    s, tab, scale, k, ku, kd, coef, cot, cot_up, cot_down, dl, st, features, pair, line
):
    t = pl.program_id(0)
    factor = 0.25 * scale[t]
    col = columns_of(s)
    norms = [Norm(coef.at[0], None, m, s.batches) for m in range(s.batches)]

    zero = jnp.zeros((s.cols, s.channels), F32)
    few = s.cols // 2

    def spread(half_row):
        value = factor * half_row.astype(F32)
        for c in range(0, s.channels, 128):
            at = c // 128 * s.cols
            line[pl.ds(at, few, stride=2), :] = value[:, c : c + 128]
            line[pl.ds(at + 1, few, stride=2), :] = value[:, c : c + 128]
        return jnp.concatenate(
            [line[row_of(c // 128, s.cols), :] for c in range(0, s.channels, 128)], axis=1
        )

    def slope(x, weight, m, i):
        scaled = norms[m].scaled(x)
        level = norms[m].level(scaled)
        q = logistic(level)
        inside = col < width_at(tab, s, m, i)
        dy = jnp.where(inside, weight * (q * (1.0 + level * (1.0 - q))), 0.0)
        dl[0, ext_slice(s, m, i), :] = dy
        return dy, scaled, jnp.where(inside, level * q, 0.0)

    for m in range(s.batches):
        at, pooled = pl.ds(m * s.cols, s.cols), pl.ds(m * few, few)
        slope(ku[0, at, :], spread(cot_up[0, pooled, :]), m, 0)
        slope(kd[0, at, :], spread(cot_down[0, pooled, :]), m, s.rows + 1)

        def step(i, totals, m=m):
            finished = None
            weight = spread(cot[0, row_of(m * (s.rows // 2) + i, few), :])
            for r in (2 * i, 2 * i + 1):
                dy, scaled, y = slope(k[0, own_slice(s, m, r), :], weight, m, r + 1)
                totals = (totals[0] + dy, totals[1] + dy * scaled)
                finished = y if finished is None else finished + y
            for c in range(0, s.channels, 128):
                pair[row_of(c // 128, s.cols), :] = finished[:, c : c + 128]
            for c in range(0, s.channels, 128):
                even = pair[pl.ds(c // 128 * s.cols, few, stride=2), :]
                odd = pair[pl.ds(c // 128 * s.cols + 1, few, stride=2), :]
                features[0, row_of(m * (s.rows // 2) + i, few), c : c + 128] = 0.25 * (even + odd)
            return totals

        totals = lax.fori_loop(0, s.rows // 2, step, (zero, zero))
        st[0, pl.ds(m, 1), :] = jnp.sum(totals[0], axis=0, keepdims=True)
        st[0, pl.ds(s.batches + m, 1), :] = jnp.sum(totals[1], axis=0, keepdims=True)


def task_back_kernel(
    s, tab, slots, dl, k, ku, kd, coef, back, e, shared, coef_e, *refs
):
    pieces, (dle, part, st, dk, x, p, w, sem) = refs[:-8], refs[-8:]
    t = pl.program_id(0)

    def copies(task):
        return fetch(s, pieces, slots, w.at[task % 2], sem.at[task % 2], 9 * task, 9)

    @pl.when(t == 0)
    def _():
        start_all(copies(0))
        part[...] = jnp.zeros_like(part)

    @pl.when(t + 1 < s.tasks)
    def _():
        start_all(copies(t + 1))

    col = columns_of(s)
    norms = [Norm(coef.at[0], back.at[0], m, s.batches) for m in range(s.batches)]

    def grad(row, m, i):
        dy = dl[0, ext_slice(s, m, i), :]
        dz = norms[m].grad(dy, norms[m].scaled(row))
        dz = jnp.where(col < width_at(tab, s, m, i), dz, 0.0).astype(BF16)
        dk[0, ext_slice(s, m, i), :] = dz
        return dz.astype(F32)

    stage(
        s,
        x,
        lambda m: grad(ku[0, pl.ds(m * s.cols, s.cols), :], m, 0),
        lambda m, r: grad(k[0, own_slice(s, m, r), :], m, r + 1),
        lambda m: grad(kd[0, pl.ds(m * s.cols, s.cols), :], m, s.rows + 1),
    )
    wait_all(copies(t))
    product(s, x, w.at[t % 2], p, True)
    wide = [Norm(coef_e.at[0], None, m, s.batches) for m in range(s.batches)]

    def slope(m, r):
        scaled = wide[m].scaled(e[0, ext_slice(s, m, r + 1), :])
        q = logistic(wide[m].level(scaled))
        att = jnp.where(col < width_at(tab, s, m, r + 1), q, 0.0)
        share = combined(s, tab, p, m, r) * att
        part[own_slice(s, m, r), :] += share
        dy = share * shared[ext_slice(s, m, r + 1), :] * (1.0 - q)
        dle[0, own_slice(s, m, r), :] = dy
        return dy, scaled

    put_gradients(s, st.at[0], slope)


def expand_back_kernel(
    s, tab, slots, dle, e, coef_e, back_e, a, coef_a, p0, p1, da, st, de, w, sem
):
    t = pl.program_id(0)
    copies = fetch(s, (p0, p1), slots, w, sem, 10, 1)

    @pl.when(t == 0)
    def _():
        start_all(copies)

    col = columns_of(s)
    norms = [Norm(coef_e.at[0], back_e.at[0], m, s.batches) for m in range(s.batches)]

    def grad(m, r):
        scaled = norms[m].scaled(e[0, ext_slice(s, m, r + 1), :])
        dz = norms[m].grad(dle[0, own_slice(s, m, r), :], scaled)
        dz = jnp.where(col < width_at(tab, s, m, r + 1), dz, 0.0)
        de[0, own_slice(s, m, r), :] = dz.astype(BF16)

    each_row(s, grad)

    @pl.when(t == 0)
    def _():
        wait_all(copies)
        da[...] = jnp.zeros_like(da)

    term = lax.dot_general(de[0], w[0], (((1,), (1,)), ((), ())), preferred_element_type=F32)
    mine = lane_task(s, (1, s.channels), 1) == t
    da[...] += jnp.where(mine, term, 0.0)

    @pl.when(t == s.tasks - 1)
    def _():
        narrow = [Norm(coef_a, None, m, s.batches) for m in range(s.batches)]

        def slope(m, r):
            scaled = narrow[m].scaled(a[ext_slice(s, m, r + 1), :])
            dy = da[own_slice(s, m, r), :] * silu_slope(narrow[m].level(scaled))
            dy = jnp.where(col < width_at(tab, s, m, r + 1), dy, 0.0)
            da[own_slice(s, m, r), :] = dy
            return dy, scaled

        put_gradients(s, st, slope)


def squeeze_back_kernel(
    s, tab, slots, dla, a, coef_a, back_a, part, z2, coef, p0, p1, dl, st, eu, ed, da, w, sem
):
    copies = fetch(s, (p0, p1), slots, w, sem, 9, 1)
    start_all(copies)
    col = columns_of(s)
    narrow = [Norm(coef_a, back_a, m, s.batches) for m in range(s.batches)]

    def grad(m, r):
        scaled = narrow[m].scaled(a[ext_slice(s, m, r + 1), :])
        dz = narrow[m].grad(dla[own_slice(s, m, r), :], scaled)
        dz = jnp.where(col < width_at(tab, s, m, r + 1), dz, 0.0)
        da[own_slice(s, m, r), :] = dz.astype(BF16)

    each_row(s, grad)
    wait_all(copies)
    dl[...] = lax.dot_general(da[...], w[0], (((1,), (1,)), ((), ())), preferred_element_type=F32)
    norms = [Norm(coef, None, m, s.batches) for m in range(s.batches)]

    def slope(m, r):
        at = own_slice(s, m, r)
        scaled = norms[m].scaled(z2[at, :])
        dy = (dl[at, :] + part[at, :]) * silu_slope(norms[m].level(scaled))
        dy = jnp.where(col < width_at(tab, s, m, r + 1), dy, 0.0)
        dl[at, :] = dy
        return dy, scaled

    put_gradients(s, st, slope)
    put_edges(s, dl, eu, ed)


def norm_rows(s, tab, dl, dlu, dld, z, zu, zd, coef, back, dz):
    col = columns_of(s)
    norms = [Norm(coef, back, m, s.batches) for m in range(s.batches)]

    def grad(dy, x, m, i):
        y = norms[m].grad(dy, norms[m].scaled(x))
        y = jnp.where(col < width_at(tab, s, m, i), y, 0.0).astype(BF16)
        dz[ext_slice(s, m, i), :] = y
        return y.astype(F32)

    def up(m):
        at = pl.ds(m * s.cols, s.cols)
        return grad(dlu[at, :], zu[at, :], m, 0)

    def down(m):
        at = pl.ds(m * s.cols, s.cols)
        return grad(dld[at, :], zd[at, :], m, s.rows + 1)

    def own(m, r):
        at = own_slice(s, m, r)
        return grad(dl[at, :], z[at, :], m, r + 1)

    return up, own, down


def kept_rows(s, dz):
    def row(m, i):
        return dz[ext_slice(s, m, i), :].astype(F32)

    return (lambda m: row(m, 0)), (lambda m, r: row(m, r + 1)), (lambda m: row(m, s.rows + 1))


def conv_two_back_kernel(
    s, tab, slots, dl, dlu, dld, z, zu, zd, coef, back, z1, coef1, p0, p1, dl1, st, eu, ed, dz, x, p, w, sem
):
    copies = fetch(s, (p0, p1), slots, w, sem, 0, 9)
    start_all(copies)
    stage(s, x, *norm_rows(s, tab, dl, dlu, dld, z, zu, zd, coef, back, dz))
    wait_all(copies)
    product(s, x, w, p, True)
    col = columns_of(s)
    norms = [Norm(coef1, None, m, s.batches) for m in range(s.batches)]

    def slope(m, r):
        scaled = norms[m].scaled(z1[own_slice(s, m, r), :])
        dy = combined(s, tab, p, m, r) * silu_slope(norms[m].level(scaled))
        dy = jnp.where(col < width_at(tab, s, m, r + 1), dy, 0.0)
        dl1[own_slice(s, m, r), :] = dy
        return dy, scaled

    put_gradients(s, st, slope)
    put_edges(s, dl1, eu, ed)


def conv_one_back_kernel(s, tab, slots, dz, p0, p1, p2, p3, out, x, p, w, sem):
    copies = fetch(s, (p0, p1, p2, p3), slots, w, sem, 0, 9)
    start_all(copies)
    stage(s, x, *kept_rows(s, dz))
    wait_all(copies)
    product(s, x, w, p, True)
    col = columns_of(s)

    def mask(m, r):
        y = combined(s, tab, p, m, r)
        out[own_slice(s, m, r), :] = jnp.where(col < width_at(tab, s, m, r + 1), y, 0.0)

    each_row(s, mask)


def put_blocks(s, slots, res, side, keep, send, tap):
    target = (keep, send)[side]
    for block in range(BLOCKS):
        rows = res[block * s.block : (block + 1) * s.block]
        target[slots[(2 + side) * BLOCKS + 2 + block], tap] = rows.astype(BF16)


def put_turned(lanes, v, vt):
    turned = v.T
    vt[0] = turned * lanes[pl.ds(0, 1), :].astype(BF16)
    vt[1] = turned
    vt[2] = turned * lanes[pl.ds(1, 1), :].astype(BF16)


def tap_products(s, slots, vt, x, keep, send):
    def one(tap, carry):
        a, b = 2 - tap // 3, 2 - tap % 3
        for side in (1, 0):
            half = row_of(2 * b + slots[2 * BLOCKS + side], s.half)
            res = None
            for m in range(s.batches):
                rows = pl.ds(pl.multiple_of(m * s.ext + a * s.cols, s.cols), s.own)
                term = jnp.dot(
                    vt[a, :, m * s.own : (m + 1) * s.own],
                    x[rows, half],
                    preferred_element_type=F32,
                )
                res = term if res is None else res + term
            put_blocks(s, slots, res, side, keep, send, tap)
        return carry

    lax.fori_loop(0, 9, one, 0)


def task_weight_kernel(s, slots, lanes, v, dz, keep, send, x, vt):
    stage(s, x, *kept_rows(s, dz.at[0]))
    put_turned(lanes, v[0], vt)
    tap_products(s, slots, vt, x, keep, send)


def conv_two_weight_kernel(
    s, slots, lanes, v, dz, shared, da, narrow, de, keep, send, x, vt
):
    stage(s, x, *kept_rows(s, dz))
    put_turned(lanes, v[...], vt)
    tap_products(s, slots, vt, x, keep, send)
    for m in range(s.batches):
        own = shared[pl.ds(m * s.ext + s.cols, s.own), :].astype(BF16)
        vt[0, :, m * s.own : (m + 1) * s.own] = own.T
    vt[1] = narrow[...].T
    owner = lane_task(s, (s.channels, s.half), 0)
    for side in (1, 0):
        half = row_of(slots[2 * BLOCKS + side], s.half)
        res = jnp.dot(vt[0], da[:, half], preferred_element_type=F32)
        put_blocks(s, slots, res, side, keep, send, 9)
        res = jnp.zeros((s.channels, s.half), F32)
        for t in range(s.tasks):
            term = jnp.dot(vt[1], de[t, :, half], preferred_element_type=F32)
            res = jnp.where(owner == t, term, res)
        put_blocks(s, slots, res, side, keep, send, 10)


def conv_one_weight_kernel(
    s, tab, slots, lanes, img, dl, dlu, dld, z, zu, zd, coef, back, keep, send, dz, x, v, vt
):
    stage(s, x, *norm_rows(s, tab, dl, dlu, dld, z, zu, zd, coef, back, dz))
    col = columns_of(s)

    def valid(m, r):
        at = own_slice(s, m, r)
        row = jnp.where(col < width_at(tab, s, m, r + 1), img[at, :].astype(F32), 0.0)
        v[at, :] = row.astype(BF16)

    each_row(s, valid)
    put_turned(lanes, v[...], vt)
    tap_products(s, slots, vt, x, keep, send)


def is_near(x, spec):
    return spec.memory_space == pltpu.VMEM and x.size * x.dtype.itemsize <= NEAR


def block_bytes(x, spec):
    if spec.block_shape is None:
        return x.size * x.dtype.itemsize if spec.memory_space == pltpu.VMEM else 0
    return 2 * math.prod(spec.block_shape) * x.dtype.itemsize


def is_far(x, spec, grid):
    if spec.memory_space == pltpu.HBM:
        return True
    part = spec.block_shape is not None and math.prod(spec.block_shape) < x.size
    return grid == (1,) and part and x.size > FAR


def placed(x, spec, grid):
    if is_far(x, spec, grid):
        return pltpu.with_memory_space_constraint(x, pltpu.HBM)
    return pltpu.with_memory_space_constraint(x, pltpu.VMEM) if is_near(x, spec) else x


def placed_shape(x, spec):
    return pltpu.VMEM(x.shape, x.dtype) if is_near(x, spec) else x


def call(kernel, s, ins, outs, scratch, grid=None, after=()):
    shapes = [shape for shape, _ in outs]
    given, extra = len(ins), len(after)

    def body(*refs):
        kernel(s, *refs[:given], *refs[given + extra :])

    ins = [(placed(x, spec, grid), spec) for x, spec in ins] + [(x, unread()) for x in after]
    options = {} if grid is None else {"grid": grid}
    room = sum(block_bytes(x, spec) for x, spec in list(ins) + list(outs))
    for ref in scratch:
        if ref.memory_space == pltpu.VMEM:
            room += math.prod(ref.shape) * jnp.dtype(ref.dtype).itemsize
    return pl.pallas_call(
        body,
        out_shape=[placed_shape(x, spec) for x, spec in outs],
        in_specs=[spec for _, spec in ins],
        out_specs=[spec for _, spec in outs],
        scratch_shapes=scratch,
        compiler_params=pltpu.CompilerParams(vmem_limit_bytes=room + SPARE),
        cost_estimate=pl.CostEstimate(flops=1024, bytes_accessed=1024, transcendentals=0),
        **options,
    )(*[x for x, _ in ins])


class Links:
    def __init__(self, dp, rep):
        self.dp, self.rep, self.count = dp, rep, dp * rep
        self.me_dp, self.me_rep = lax.axis_index("dp"), lax.axis_index("rep")
        self.me = self.me_dp * rep + self.me_rep
        bits = (self.count - 1).bit_length()
        self.groups = [(1,)]
        for bit in range(1, bits, 2):
            low = 1 << bit
            self.groups.append((low,) if bit + 1 == bits else (low, 2 * low, 3 * low))
        self.direct = dp == BLOCKS and rep == 2
        self.column = ((16, 16), (8, 8), (24, 24))
        self.steps = ((4, 2), (2, 4))
        self.ring = list(range(dp))
        if self.direct:
            self.ring = [
                4 * (z if i % 2 == 0 else 3 - z) + column
                for i, column in enumerate((0, 1, 3, 2))
                for z in range(4)
            ]

    def swap(self, x, masks):
        pairs = [(i, i ^ masks[i % 2]) for i in range(self.count)]
        return lax.ppermute(x, AXES, pairs)

    def shift(self, x, by):
        pairs = [(i, i + by) for i in range(self.count) if 0 <= i + by < self.count]
        return lax.ppermute(x, AXES, pairs)

    def neighbours(self, top, bottom):
        return self.shift(bottom, 1), self.shift(top, -1)


def total_of(items):
    if len(items) == 2:
        return items[0] + items[1]
    return (items[0] + items[1]) + (items[2] + items[3])


def group_counts(links, counts):
    places = jnp.arange(links.count, dtype=jnp.int32)[None, :]

    def among(place, low):
        same = (places | low) == (place | low)
        return jnp.sum(jnp.where(same, counts, 0.0), axis=1, keepdims=True)

    return [
        [among(links.me ^ mask, group[0] - 1) for mask in (0, *group)] for group in links.groups
    ]


def statistics_over(links, st, stages, batches, gain, shift):
    tasks, _, channels = st.shape
    given = []
    for group, counts in zip(links.groups, stages):
        met = [st] + [links.swap(st, (mask, mask)) for mask in group]
        count = total_of(counts)
        total = total_of([x[:, :batches] for x in met])
        mean = total / count
        spread = total_of(
            [x[:, batches:] + n * (x[:, :batches] / n - mean) ** 2 for x, n in zip(met, counts)]
        )
        st = jnp.concatenate([total, spread], axis=1)
        given.append(st)
    mean = st[:, :batches] / count
    inverse = lax.rsqrt(st[:, batches:] / count + EPSILON)
    wide = (tasks, batches, channels)
    coef = jnp.concatenate(
        [
            mean,
            inverse,
            jnp.broadcast_to(gain[:, None], wide),
            jnp.broadcast_to(shift[:, None], wide),
        ],
        axis=1,
    )
    return coef, given


def sums_over(links, st, between=None):
    given = []
    for i, group in enumerate(links.groups):
        st = total_of([st] + [links.swap(st, (mask, mask)) for mask in group])
        given.append(st)
        if i == 1 and between is not None:
            extra = between(given)
            st = tied(st, extra) if extra else st
    return st, given


def join_kernel(s, *refs):
    at = 0
    for ref in refs[:-1]:
        refs[-1][pl.ds(at, ref.shape[0])] = ref[...]
        at += ref.shape[0]


def tied(x, after):
    count = len(after)
    return pl.pallas_call(
        lambda *refs: None,
        out_shape=jax.ShapeDtypeStruct(x.shape, x.dtype),
        in_specs=[unread()] * (1 + count),
        out_specs=unread(),
        input_output_aliases={0: 0},
    )(x, *after)


def joined(arrays, after=()):
    shape = (sum(x.shape[0] for x in arrays), *arrays[0].shape[1:])
    return call(
        join_kernel,
        None,
        [(x, whole()) for x in arrays],
        [(jax.ShapeDtypeStruct(shape, arrays[0].dtype), whole())],
        [],
        after=after,
    )[0]


class Gather:
    def __init__(self, links, block, after_z=()):
        self.links = links
        half = block.shape[2] // 2
        mine = lax.dynamic_slice_in_dim(block, links.me_rep * half, half, axis=2)[None]
        self.own = joined([mine], after_z) if after_z else mine
        self.along = [links.swap(self.own, masks) for masks in links.column]

    def across(self, after=()):
        self.four = joined([self.own, *self.along], after)
        self.fourth = self.links.swap(self.four, self.links.steps[0])
        return self.four

    def finish(self, after=()):
        links = self.links
        self.mine = joined([self.four, self.fourth], after)
        self.more = links.swap(self.mine, links.steps[1])
        self.pieces = [
            self.mine,
            self.more,
            links.swap(self.mine, (1, 1)),
            links.swap(self.more, (1, 1)),
        ]
        return self.mine


def gather_halves(links, block, order):
    half = block.shape[2] // 2
    mine = lax.dynamic_slice_in_dim(block, links.me_rep * half, half, axis=2)
    return lax.all_gather(mine, "dp", axis_index_groups=order)


def split_blocks(full, parts):
    slabs, rows, cols = full.shape
    x = full.reshape(slabs, BLOCKS, rows // BLOCKS, 2, cols // 2)
    x = jnp.transpose(x, (3, 1, 0, 2, 4))
    size = BLOCKS // parts
    return [x[side, i * size : (i + 1) * size] for side in range(2) for i in range(parts)]


def slot_table(links):
    places = jnp.arange(BLOCKS, dtype=jnp.int32)
    if not links.direct:
        return jnp.concatenate([places, places, jnp.array([0, 1], jnp.int32), places, places])
    tables = []
    for core in range(2):
        offsets = [0] + [masks[core] // 2 for masks in links.column]
        for masks in links.steps:
            offsets = offsets + [o ^ (masks[core] // 2) for o in offsets]
        tables.append(offsets)
    inverse = [[t.index(o) for o in range(BLOCKS)] for t in tables]
    first = links.me_rep == 0
    me = links.me_dp
    ours = jnp.where(first, jnp.array(tables[0], jnp.int32), jnp.array(tables[1], jnp.int32))
    theirs = jnp.where(first, jnp.array(tables[1], jnp.int32), jnp.array(tables[0], jnp.int32))
    back = [jnp.array(t, jnp.int32) for t in inverse]
    offset = me ^ places
    match = (offset[:, None] == places[None, :]).astype(jnp.int32)
    slot = [
        jnp.sum(match * jnp.where(first, back[i], back[1 - i])[None, :], axis=1) for i in range(2)
    ]
    halves = jnp.stack([links.me_rep, 1 - links.me_rep]).astype(jnp.int32)
    return jnp.concatenate([me ^ ours, me ^ theirs, halves, *slot]).astype(jnp.int32)


def fold_kernel(s, *refs):
    total = refs[0][...].astype(F32)
    for ref in refs[1:-1]:
        total = total + ref[...].astype(F32)
    refs[-1][...] = total.astype(BF16)


class Scatter:
    def __init__(self, links, keep, send):
        self.links, self.keep, self.send = links, keep, send
        self.parts, self.count = [keep], BLOCKS
        if links.direct:
            self.got = ()
        else:
            self.full = join_blocks(keep, send)
            self.got = ()

    def start(self, after=()):
        if self.links.direct:
            send = tied(self.send, after) if after else self.send
            self.parts.append(self.links.swap(send, (1, 1)))
        return self

    def step(self, after=()):
        links = self.links
        if not links.direct:
            return ()
        self.count //= 2
        count, shape = self.count, self.keep.shape[1:]
        (out,) = call(
            fold_kernel,
            None,
            [(part, pl.BlockSpec((count, *shape), lambda i: (1, 0, 0, 0))) for part in self.parts],
            [
                (
                    jax.ShapeDtypeStruct((count, *shape), BF16),
                    pl.BlockSpec((count, *shape), lambda i: (0, 0, 0, 0)),
                )
            ],
            [],
            grid=(1,),
            after=after,
        )
        self.got = (links.swap(out, links.steps[1 if count == 8 else 0]),)
        self.parts.extend(self.got)
        return (out,)


def column_kernel(s, *refs, counts):
    ins, outs = refs[:-4], refs[-4:]
    first, at = 0, 0
    for count in counts:
        slabs = ins[first].shape[1]
        for i, out in enumerate(outs):
            total = None
            for ref in ins[first : first + count]:
                term = ref[i].astype(F32)
                total = term if total is None else total + term
            out[pl.ds(at, slabs)] = total.astype(out.dtype)
        first, at = first + count, at + slabs


class Column:
    def __init__(self, links, units, after=()):
        self.links = links
        block = units[0].keep.shape[2:]
        slabs = sum(unit.keep.shape[1] for unit in units)
        ins = []
        for unit in units:
            spec = pl.BlockSpec((4, *unit.keep.shape[1:]), lambda i: (0, 0, 0, 0))
            ins.extend((part, spec) for part in unit.parts)
        spec = pl.BlockSpec((slabs, *block), lambda i: (0, 0, 0))
        kinds = (F32, BF16, BF16, BF16)
        self.own, *self.out = call(
            functools.partial(column_kernel, counts=[len(unit.parts) for unit in units]),
            None,
            ins,
            [(jax.ShapeDtypeStruct((slabs, *block), kind), spec) for kind in kinds],
            [],
            grid=(1,),
            after=after,
        )
        self.got = [links.swap(x, masks) for x, masks in zip(self.out, links.column)]

    def rows(self, after=()):
        mine = tied(self.own, after) if after else self.own
        for part in self.got:
            mine = mine + part.astype(F32)
        return join_halves(self.links, mine)


def join_halves(links, mine):
    other = links.swap(mine, (1, 1)).astype(F32)
    mine = mine.astype(F32)
    first = links.me_rep == 0
    return jnp.concatenate(
        [jnp.where(first, mine, other), jnp.where(first, other, mine)], axis=-1
    )


def join_blocks(keep, send):
    x = jnp.concatenate([keep, send], axis=-1).astype(F32)
    x = jnp.transpose(x, (1, 0, 2, 3))
    return x.reshape(x.shape[0], x.shape[1] * x.shape[2], x.shape[3])


def summed_shard(x, dim):
    return lax.psum(lax.psum_scatter(x, "dp", scatter_dimension=dim, tiled=True), "rep")


def bottleneck_row(x, channels):
    tasks, width = x.shape
    x = x.reshape(tasks, width // 8, 8)
    x = jnp.pad(x, ((0, channels // width - tasks), (0, 0), (0, 0)))
    return jnp.transpose(x, (1, 0, 2)).reshape(1, channels)


def bottleneck_lanes(x, channels):
    tasks, rows, width = x.shape
    x = x.reshape(tasks, rows, width // 8, 8)
    x = jnp.pad(x, ((0, channels // width - tasks), (0, 0), (0, 0), (0, 0)))
    return jnp.transpose(x, (1, 2, 0, 3)).reshape(rows, channels)


def lanes_to_tasks(x, tasks):
    rows, channels = x.shape
    x = x.reshape(rows, channels // 32, 4, 8)[:, :, :tasks]
    return jnp.transpose(x, (2, 0, 1, 3)).reshape(tasks, rows, channels // 4)


def tables(lengths, widths, offset, rows, total, cols):
    ends = 2 * jnp.cumsum(lengths, axis=1)
    starts = ends - 2 * lengths

    def width_of(places):
        before = (places[None, :, None] < ends[:, None, :]) & (
            places[None, :, None] >= starts[:, None, :]
        )
        return jnp.sum(before.astype(jnp.int32) * widths[:, None, :], axis=2)

    near = offset - 1 + jnp.arange(rows + 2, dtype=jnp.int32)
    below = offset + jnp.arange(rows + 1, dtype=jnp.int32)
    first = jnp.sum((below[None, :, None] == starts[:, None, :]).astype(jnp.int32), axis=2)
    tab = jnp.concatenate([width_of(near).reshape(-1), (1 - first).reshape(-1)])
    linked = (1 - first).astype(F32)
    lanes = jnp.stack([linked[:, :-1], linked[:, 1:]])
    lanes = jnp.repeat(lanes, cols, axis=2).reshape(2, -1)
    return tab, lanes, width_of(jnp.arange(total, dtype=jnp.int32))


def local(
    dp,
    rep,
    images,
    lengths,
    widths,
    conv_one,
    conv_two,
    squeeze,
    expand,
    task_conv,
    gains_shared,
    biases_shared,
    gains_squeeze,
    biases_squeeze,
    gains_expand,
    biases_expand,
    gains_task,
    biases_task,
    loss_history,
    cotangent,
):
    batches, rows, cols, channels = images.shape
    tasks = cotangent.shape[0]
    s = Sizes(batches, rows, cols, channels, tasks)
    links = Links(dp, rep)
    pixels, edge = batches * s.own, batches * cols
    ext = batches * s.ext

    def f32(*shape):
        return jax.ShapeDtypeStruct(shape, F32)

    def b16(*shape):
        return jax.ShapeDtypeStruct(shape, BF16)

    slots = slot_table(links)
    places = jnp.arange(BLOCKS, dtype=jnp.int32)
    ring = jnp.array(links.ring, jnp.int32) if links.direct else places
    halves = slots[2 * BLOCKS : 2 * BLOCKS + 2]
    plain = jnp.concatenate([places, places, halves])
    around = jnp.concatenate([ring, ring, halves])
    shard = conv_one.shape[2]
    if links.direct:
        narrow_rows = bottleneck_lanes(squeeze, channels)[None]
        wide_rows = jnp.pad(
            expand.reshape(-1, channels), ((0, shard - tasks * expand.shape[1]), (0, 0))
        )[None]
        two_mine = gather_halves(
            links,
            jnp.concatenate([conv_two.reshape(9, shard, channels), narrow_rows, wide_rows], axis=0),
            None,
        )
        task_rows = task_conv.reshape(9 * tasks, shard, channels)
        task_mine = gather_halves(links, task_rows, [links.ring])
        first = Gather(links, conv_one.reshape(9, shard, channels))
        first.across()
        first.finish()
        one = first.pieces
    else:
        full = lax.all_gather(conv_one, "dp", axis=2, tiled=True)
        one = split_blocks(full.reshape(9, channels, channels), 2)
        full = lax.all_gather(conv_two, "dp", axis=2, tiled=True).reshape(9, channels, channels)
        narrow_rows = bottleneck_lanes(lax.all_gather(squeeze, "dp", axis=1, tiled=True), channels)
        wide_rows = lax.all_gather(expand, "dp", axis=1, tiled=True)
        wide_rows = bottleneck_lanes(jnp.transpose(wide_rows, (0, 2, 1)), channels).T
        two = split_blocks(jnp.concatenate([full, narrow_rows[None], wide_rows[None]], axis=0), 1)
        full = lax.all_gather(task_conv, "dp", axis=3, tiled=True)
        three = split_blocks(full.reshape(9 * tasks, channels, channels), 1)

    tab, lanes, all_widths = tables(lengths, widths, links.me * rows, rows, links.count * rows, cols)
    counts = jnp.sum(all_widths.reshape(batches, links.count, rows).astype(F32), axis=2)
    stages = group_counts(links, counts)
    pixel_count = jnp.sum(counts, axis=1, keepdims=True)
    twice_count = jnp.concatenate([pixel_count, pixel_count], axis=0)
    loss_ratio = loss_history[:, 1] / loss_history[:, 0]
    task_scale = tasks * jax.nn.softmax(loss_ratio / 2.0)

    img = images.reshape(pixels, channels)
    img_up, img_down = links.neighbours(
        images[:, 0].reshape(edge, channels), images[:, -1].reshape(edge, channels)
    )
    cot_up, cot_down = links.neighbours(cotangent[:, :, :1], cotangent[:, :, -1:])
    cot = cotangent.reshape(tasks, pixels // 4, channels)
    cot_up, cot_down = (x.reshape(tasks, edge // 2, channels) for x in (cot_up, cot_down))

    pieces = [in_place()] * 4
    span = span_of(s)
    shifts = pltpu.VMEM((ext, 3 * channels), BF16)
    sums = pltpu.VMEM((3, span, channels), F32)
    weights = pltpu.VMEM((9, channels, channels), BF16)
    matrix = pltpu.VMEM((1, channels, channels), BF16)
    sems = pltpu.SemaphoreType.DMA((2 * BLOCKS,))

    def sync(st, gain, shift):
        return statistics_over(links, st, stages, batches, gain, shift)

    st_shape, edge_shape = f32(2 * batches, channels), f32(edge, channels)

    z1, st, eu, ed = call(
        conv_one_kernel,
        s,
        [(tab, scalars()), (slots, scalars()), (img, whole()), (img_up, whole()), (img_down, whole())]
        + list(zip(one, pieces)),
        [(f32(pixels, channels), whole()), (st_shape, whole()), (edge_shape, whole()), (edge_shape, whole())],
        [shifts, sums, weights, sems],
    )
    z1_up, z1_down = links.neighbours(eu, ed)
    coef1, given = sync(st[None], gains_shared[0:1], biases_shared[0:1])
    coef1 = coef1[0]
    if links.direct:
        two_mine = tied(two_mine, (given[-1],))
        two = [two_mine, links.swap(two_mine, (1, 1))]

    z2, st, eu, ed, hidden = call(
        conv_two_kernel,
        s,
        [(tab, scalars()), (plain, scalars())]
        + [(x, whole()) for x in (z1, z1_up, z1_down, coef1)]
        + list(zip(two, pieces)),
        [(f32(pixels, channels), whole()), (st_shape, whole()), (edge_shape, whole()), (edge_shape, whole()), (b16(pixels, channels), whole())],
        [shifts, sums, weights, sems],
        after=(cot_up, cot_down),
    )
    z2_up, z2_down = links.neighbours(eu, ed)
    coef2, _ = sync(st[None], gains_shared[1:2], biases_shared[1:2])
    coef2 = coef2[0]

    shared, a, st = call(
        squeeze_kernel,
        s,
        [(tab, scalars()), (plain, scalars())]
        + [(x, whole()) for x in (z2, z2_up, z2_down, coef2)]
        + list(zip(two, pieces)),
        [(f32(ext, channels), whole()), (f32(ext, channels), whole()), (st_shape, whole())],
        [pltpu.VMEM((ext, channels), BF16), matrix, sems],
    )
    coef_a, _ = sync(
        st[None], bottleneck_row(gains_squeeze, channels), bottleneck_row(biases_squeeze, channels)
    )
    coef_a = coef_a[0]

    grid = (tasks,)
    whole_task = functools.partial(
        lambda *shape: pl.BlockSpec(shape, lambda t: tuple(0 for _ in shape))
    )
    ext_task, own_task, edge_task = (
        per_task(ext, channels),
        per_task(pixels, channels),
        per_task(edge, channels),
    )
    st_task, coef_task = per_task(2 * batches, channels), per_task(4 * batches, channels)
    ext_all, own_all = whole_task(ext, channels), whole_task(pixels, channels)
    st_all, coef_all = whole_task(2 * batches, channels), whole_task(4 * batches, channels)
    edge_all = whole_task(edge, channels)

    e, st, narrow = call(
        expand_kernel,
        s,
        [(tab, scalars()), (plain, scalars()), (a, ext_all), (coef_a, coef_all)]
        + list(zip(two, pieces)),
        [(f32(tasks, ext, channels), ext_task), (f32(tasks, 2 * batches, channels), st_task), (b16(pixels, channels), own_all)],
        [pltpu.VMEM((ext, channels), BF16), matrix, sems],
        grid=grid,
    )
    coef_e, given = sync(st, gains_expand, biases_expand)
    if links.direct:
        task_mine = tied(task_mine, (given[1],))
        three = [task_mine, links.swap(task_mine, (1, 1))]

    pair = [shifts, sums, pltpu.VMEM((2, 9, channels, channels), BF16), pltpu.SemaphoreType.DMA((2, 2 * BLOCKS))]
    k, st, eu, ed, gated = call(
        task_kernel,
        s,
        [(tab, scalars()), (around, scalars()), (e, ext_task), (shared, ext_all), (coef_e, coef_task)]
        + [(x, in_place()) for x in three],
        [
            (f32(tasks, pixels, channels), own_task),
            (f32(tasks, 2 * batches, channels), st_task),
            (f32(tasks, edge, channels), edge_task),
            (f32(tasks, edge, channels), edge_task),
            (b16(tasks, pixels, channels), own_task),
        ],
        pair,
        grid=grid,
    )
    k_up, k_down = links.neighbours(eu, ed)
    coef_k, _ = sync(st, gains_task, biases_task)

    dlk, st, pooled = call(
        task_slope_kernel,
        s,
        [(tab, scalars()), (task_scale, scalars()), (k, own_task), (k_up, edge_task), (k_down, edge_task), (coef_k, coef_task), (cot, per_task(pixels // 4, channels)), (cot_up, per_task(edge // 2, channels)), (cot_down, per_task(edge // 2, channels))],
        [
            (f32(tasks, ext, channels), ext_task),
            (f32(tasks, 2 * batches, channels), st_task),
            (f32(tasks, pixels // 4, channels), per_task(pixels // 4, channels)),
        ],
        [pltpu.VMEM((channels // 128 * cols, 128), F32)] * 2,
        grid=grid,
    )
    sums_k, _ = sums_over(links, st)
    back_k = sums_k / twice_count

    dle, part, st, dk = call(
        task_back_kernel,
        s,
        [
            (tab, scalars()),
            (around, scalars()),
            (dlk, ext_task),
            (k, own_task),
            (k_up, edge_task),
            (k_down, edge_task),
            (coef_k, coef_task),
            (back_k, st_task),
            (e, ext_task),
            (shared, ext_all),
            (coef_e, coef_task),
        ]
        + [(x, in_place()) for x in three],
        [
            (f32(tasks, pixels, channels), own_task),
            (f32(pixels, channels), own_all),
            (f32(tasks, 2 * batches, channels), st_task),
            (b16(tasks, ext, channels), ext_task),
        ],
        pair,
        grid=grid,
    )
    sums_e, given = sums_over(links, st)
    back_e = sums_e / twice_count

    def outputs(slabs):
        return b16(BLOCKS, slabs, s.block, s.half)

    turned = pltpu.VMEM((3, channels, pixels), BF16)

    def task_weights(t, after):
        def at(*shape):
            return pl.BlockSpec((1, *shape), lambda i: (t, *(0 for _ in shape)))

        keep, send = call(
            task_weight_kernel,
            s,
            [(slots, scalars()), (lanes, whole_task(2, pixels)), (gated, at(pixels, channels)), (dk, at(ext, channels))],
            [(outputs(9), whole_task(BLOCKS, 9, s.block, s.half))] * 2,
            [shifts, turned],
            grid=(1,),
            after=after,
        )
        return Scatter(links, keep, send)

    task_0 = task_weights(0, (given[0],)).start()
    wait_e = (task_0.keep,)

    dla, st, de = call(
        expand_back_kernel,
        s,
        [
            (tab, scalars()),
            (plain, scalars()),
            (dle, own_task),
            (e, ext_task),
            (coef_e, coef_task),
            (back_e, st_task),
            (a, ext_all),
            (coef_a, coef_all),
        ]
        + list(zip(two, pieces)),
        [(f32(pixels, channels), own_all), (st_shape, st_all), (b16(tasks, pixels, channels), own_task)],
        [matrix, sems],
        grid=grid,
        after=wait_e,
    )
    sums_a, given = sums_over(links, st[None], lambda given: task_0.step((given[1],)))
    sums_a = sums_a[0]
    back_a = sums_a / twice_count
    task_1 = task_weights(1, (given[-1],))
    wait_a = task_0.step((given[-1], task_1.keep))

    dl2, st, eu, ed, da = call(
        squeeze_back_kernel,
        s,
        [(tab, scalars()), (plain, scalars())]
        + [(x, whole()) for x in (dla, a, coef_a, back_a, part, z2, coef2)]
        + list(zip(two, pieces)),
        [(f32(pixels, channels), whole()), (st_shape, whole()), (edge_shape, whole()), (edge_shape, whole()), (b16(pixels, channels), whole())],
        [matrix, sems],
        after=wait_a,
    )
    dl2_up, dl2_down = links.neighbours(eu, ed)
    sums_2, given = sums_over(
        links,
        st[None],
        lambda given: task_1.start((given[0],)).step((given[1], *task_0.got)),
    )
    sums_2 = sums_2[0]
    back_2 = sums_2 / twice_count
    task_2 = task_weights(2, (given[-1],))
    wait_b = task_1.step((given[-1], dl2_up, dl2_down, task_2.keep))

    dl1, st, eu, ed, dz2 = call(
        conv_two_back_kernel,
        s,
        [(tab, scalars()), (plain, scalars())]
        + [(x, whole()) for x in (dl2, dl2_up, dl2_down, z2, z2_up, z2_down, coef2, back_2, z1, coef1)]
        + list(zip(two, pieces)),
        [(f32(pixels, channels), whole()), (st_shape, whole()), (edge_shape, whole()), (edge_shape, whole()), (b16(ext, channels), whole())],
        [shifts, sums, weights, sems],
        after=wait_b,
    )
    dl1_up, dl1_down = links.neighbours(eu, ed)
    sums_1, given = sums_over(
        links,
        st[None],
        lambda given: task_2.start((given[0],)).step((given[1], *task_1.got)),
    )
    sums_1 = sums_1[0]
    back_1 = sums_1 / twice_count

    grad_two = call(
        conv_two_weight_kernel,
        s,
        [(slots, scalars()), (lanes, whole())]
        + [(x, whole()) for x in (hidden, dz2, shared, da, narrow, de)],
        [(outputs(11), whole()), (outputs(11), whole())],
        [shifts, turned],
        after=(given[-1],),
    )
    two_sums = Scatter(links, *grad_two)
    wait_c = task_2.step((given[-1], dl1_up, dl1_down, two_sums.keep))
    two_sums.start(wait_c)
    task_sums = (task_0, task_1, task_2)

    keep, send, dz1 = call(
        conv_one_weight_kernel,
        s,
        [(tab, scalars()), (slots, scalars()), (lanes, whole())]
        + [(x, whole()) for x in (img, dl1, dl1_up, dl1_down, z1, z1_up, z1_down, coef1, back_1)],
        [(outputs(9), whole()), (outputs(9), whole()), (b16(ext, channels), whole())],
        [shifts, pltpu.VMEM((pixels, channels), BF16), turned],
        after=wait_c,
    )
    one_sums = Scatter(links, keep, send)
    wait_d = ()
    if links.direct:
        task_column = Column(links, task_sums, (dz1,))
        one_sums.start(task_column.out[:1])
        wait_d = one_sums.step(two_sums.step(task_column.out))

    (input_grad,) = call(
        conv_one_back_kernel,
        s,
        [(tab, scalars()), (slots, scalars()), (dz1, whole())] + list(zip(one, pieces)),
        [(f32(pixels, channels), whole())],
        [shifts, sums, weights, sems],
        after=wait_d,
    )

    width = squeeze.shape[2]
    if links.direct:
        order = two_sums.step((input_grad,))
        one_sums.step(order)
        last_column = Column(links, (one_sums, two_sums))
        three_rows = task_column.rows()
        last_rows = last_column.rows()
        one_rows, two_rows = last_rows[:9], last_rows[9:]
        grad_squeeze = lanes_to_tasks(two_rows[9], tasks)
        grad_expand = two_rows[10].reshape(4, expand.shape[1], channels)[:tasks]
    else:
        three_rows = summed_shard(jnp.concatenate([part.full for part in task_sums], axis=0), 1)
        full = two_sums.full
        two_rows = summed_shard(full[:9], 1)
        one_rows = summed_shard(one_sums.full, 1)
        grad_squeeze = summed_shard(lanes_to_tasks(full[9], tasks), 1)
        wide = jnp.transpose(lanes_to_tasks(full[10].T, tasks), (0, 2, 1))
        grad_expand = summed_shard(wide, 1)

    def both(sums):
        shift = sum(sums[..., m, :] for m in range(batches))
        gain = sum(sums[..., batches + m, :] for m in range(batches))
        return gain, shift

    gain_1, shift_1 = both(sums_1)
    gain_2, shift_2 = both(sums_2)
    gain_a, shift_a = both(sums_a)
    gain_e, shift_e = both(sums_e)
    gain_k, shift_k = both(sums_k)

    def tasks_row(x):
        return lanes_to_tasks(x[None], tasks).reshape(tasks, width)

    return (
        pooled.reshape(cotangent.shape),
        input_grad.reshape(images.shape),
        one_rows.reshape(conv_one.shape),
        two_rows[:9].reshape(conv_two.shape),
        grad_squeeze,
        grad_expand,
        three_rows.reshape(task_conv.shape),
        jnp.stack([gain_1, gain_2]),
        jnp.stack([shift_1, shift_2]),
        tasks_row(gain_a),
        tasks_row(shift_a),
        gain_e,
        shift_e,
        gain_k,
        shift_k,
    )


def solution(mesh):
    rows = P(None, AXES, None, None)
    pooled = P(None, None, AXES, None, None)
    conv = P(None, None, "dp", None)
    small = P(None, "dp", None)
    task = P(None, None, None, "dp", None)
    rest = P()
    return jax.shard_map(
        functools.partial(local, mesh.shape["dp"], mesh.shape["rep"]),
        mesh=mesh,
        in_specs=(rows, rest, rest, conv, conv, small, small, task) + (rest,) * 9 + (pooled,),
        out_specs=(pooled, rows, conv, conv, small, small, task) + (rest,) * 8,
        check_vma=False,
    )
```
